32 devices in a mesh: slab: 2 (over x), scan: 8 (over z, y), mz: 2 (over core).
Axes of the slice: x: 2, y: 2, z: 4, core: 2. Of those that a mesh axis runs over, the one named last changes fastest.
Arguments:
- spectra: bfloat16 [12288, 8192], P('mz', ('slab', 'scan')), parts along dimension 1, may hold values from 0 to 1
- templates: bfloat16 [2, 12288, 512], P('mz', ('slab', 'scan')), parts along dimension 1, may hold values from 0 to 2
- activations: float32 [64, 8192], P(None, ('slab', 'scan')), parts along dimension 1, may hold values from 0 to 1
- h_rate: float32 [64], replicated, may hold values from 0.02 to 0.08
- w_rate: float32 [64], replicated, may hold values from 0.2 to 0.8
Outputs:
- new_activations: float32 [64, 8192], P(None, ('slab', 'scan')), parts along dimension 1
- new_templates: bfloat16 [2, 12288, 512], P('mz', ('slab', 'scan')), parts along dimension 1
The draws below stay inside these ranges and needn't reach their ends.
There are 2 independent parts, one for each index of `slab`. The reference program is written for one: setup_inputs(seed, part) draws one part's arguments, and reference() takes and returns one part's arrays. A program takes and returns all parts, laid end to end along the dimension named above; an argument that names none is the same for every part. Nothing has to cross between parts.
All inputs are finite; a program needn't handle non-finite values.
Results may differ from the reference program's by a relative error of at most 0.00082.
Values may be sent and summed in bfloat16 or wider, within the bound.
A program may use at most 128 MiB of HBM per device.

```python
import math
import jax
import jax.numpy as jnp
from jax import lax

M = 12288
K = 64
LAGS = 8
LAG = 64
SCAN_DEV = 512
SPAN = 448
SCANS = 4096
N_SCAN = 8
N_MZ = 2


def unit_values(key, shape):
    return jax.random.uniform(key, shape, jnp.float32, 0.0, 1.0)


def draw_spectra(key, part):
    inner = jax.random.fold_in(key, 11)
    return unit_values(inner, (M, SCAN_DEV * N_SCAN)).astype(jnp.bfloat16)


def draw_templates(key, part):
    inner = jax.random.fold_in(key, 23)
    return (2.0 * unit_values(inner, (N_MZ, M // N_MZ, LAGS * K))).astype(jnp.bfloat16)


def draw_activations(key, part):
    inner = jax.random.fold_in(key, 37)
    return unit_values(inner, (K, SCAN_DEV * N_SCAN)).astype(jnp.float32)


def setup_inputs(seed: int = 0, part: int = 0) -> dict:
    key_of = jax.random.split(jax.random.key(seed), 6)
    part_splits = jax.random.split(jax.random.fold_in(key_of[5], part), 6)
    spectra = draw_spectra(jax.random.fold_in(jax.random.fold_in(key_of[5], part), 71), part)
    templates = draw_templates(jax.random.fold_in(jax.random.fold_in(key_of[5], part), 71), part)
    activations = draw_activations(jax.random.fold_in(jax.random.fold_in(key_of[5], part), 71), part)
    h_rate = jnp.clip(jnp.exp(jax.random.uniform(key_of[3], (K,), jnp.float32, math.log(0.02), math.log(0.08))), 0.02, 0.08)
    w_rate = jnp.clip(jnp.exp(jax.random.uniform(key_of[4], (K,), jnp.float32, math.log(0.2), math.log(0.8))), 0.2, 0.8)
    return {"spectra": spectra, "templates": templates, "activations": activations, "h_rate": h_rate, "w_rate": w_rate}


def lagged(hb):
    padded = jnp.pad(hb, ((0, 0), (SPAN, 0)))
    return jnp.concatenate([padded[:, SPAN - l * LAG:SPAN - l * LAG + SCANS] for l in range(LAGS)], 0)


def product(a, b):
    return jnp.dot(a.astype(jnp.float32), b.astype(jnp.float32), precision=lax.Precision.HIGHEST)


def reference(spectra, templates, activations, h_rate, w_rate):
    scale = 1.0 / (LAGS * K)
    weights = templates.reshape(M, LAGS * K)
    data = spectra.astype(jnp.float32)
    stack = lagged(activations.astype(jnp.bfloat16))
    resid = (scale * product(weights, stack) - data).astype(jnp.bfloat16)
    prods = product(weights.T, resid)
    padded = jnp.pad(prods, ((0, 0), (0, SPAN)))
    grad_h = padded[0:K, 0:SCANS]
    for l in range(1, LAGS):
        grad_h = grad_h + padded[l * K:(l + 1) * K, l * LAG:l * LAG + SCANS]
    grad_h = scale * grad_h
    new_h = jnp.maximum(activations - h_rate[:, None] * grad_h, 0.0)
    stack_new = lagged(new_h.astype(jnp.bfloat16))
    resid_new = (scale * product(weights, stack_new) - data).astype(jnp.bfloat16)
    grad_w = scale * product(resid_new, stack_new.T)
    rates = jnp.tile(w_rate, LAGS)[None, :]
    new_w = jnp.maximum(weights.astype(jnp.float32) - rates * grad_w, 0.0).astype(jnp.bfloat16)
    return new_h, new_w.reshape(N_MZ, M // N_MZ, LAGS * K)
```

```python
import functools

import jax
import jax.numpy as jnp
from jax import lax
from jax.experimental import pallas as pl
from jax.experimental.pallas import tpu as pltpu
from jax.sharding import PartitionSpec as P

K = 64
LAGS = 8
LAG = 64
LANES = 128
F32 = jnp.float32
BF16 = jnp.bfloat16
MESH = pl.DeviceIdType.MESH


def crossed(a, b, n):
    out, bit = 0, 1
    while bit < n:
        out = out + bit * ((a // bit + b // bit) % 2)
        bit *= 2
    return out


def kernel(
    n, chunks, spectra, w_ref, act_ref, h_rate, w_rate, h_out, w_out,
    sbuf, hraw, stack, gacc, gfin, from_core, gsum, from_scan, nh, hn, total_w,
    own_sem, s_send, s_recv, h_send, h_recv, a_sem, b_send, b_recv, c_send, c_recv, d_sem, e_sem,
):
    rows, width = sbuf.shape[1], sbuf.shape[2]
    half = width // 2
    step = rows // chunks
    scale = 1.0 / (LAGS * K)
    i = lax.axis_index("scan")
    mz = lax.axis_index("mz")
    other = 1 - mz
    two = n & (n - 1) == 0

    def to(d):
        return crossed(i, d, n) if two else lax.rem(i + d, n)

    def source(d):
        return crossed(i, d, n) if two else lax.rem(i + n - d, n)

    def each(body, start=1):
        def run(d, carry):
            body(d)
            return carry

        lax.fori_loop(start, n, run, 0)

    barrier = pltpu.get_barrier_semaphore()
    each(lambda d: pl.semaphore_signal(barrier, inc=1, device_id={"scan": to(d)}, device_id_type=MESH))
    pl.semaphore_signal(barrier, inc=1, device_id={"mz": other}, device_id_type=MESH)
    hraw[i] = act_ref[...].astype(BF16)
    pl.semaphore_wait(barrier, n)

    def send_h(d):
        return pltpu.make_async_remote_copy(
            src_ref=hraw.at[i], dst_ref=hraw.at[i], send_sem=h_send.at[d], recv_sem=h_recv.at[i],
            device_id={"scan": to(d)}, device_id_type=MESH,
        )

    def land_h(d):
        return pltpu.make_async_remote_copy(
            src_ref=hraw.at[source(d)], dst_ref=hraw.at[source(d)], send_sem=h_send.at[d],
            recv_sem=h_recv.at[source(d)], device_id={"scan": to(d)}, device_id_type=MESH,
        )

    def send_s(c, d):
        return pltpu.make_async_remote_copy(
            src_ref=spectra.at[pl.ds(pl.multiple_of(to(d) * rows + c * step, step), step), :],
            dst_ref=sbuf.at[i, pl.ds(c * step, step), :],
            send_sem=s_send.at[c, d], recv_sem=s_recv.at[c, i],
            device_id={"scan": to(d)}, device_id_type=MESH,
        )

    def land_s(c, d):
        return pltpu.make_async_remote_copy(
            src_ref=spectra.at[pl.ds(c * step, step), :],
            dst_ref=sbuf.at[source(d), pl.ds(c * step, step), :],
            send_sem=s_send.at[c, d], recv_sem=s_recv.at[c, source(d)],
            device_id={"scan": to(d)}, device_id_type=MESH,
        )

    own = pltpu.make_async_copy(
        spectra.at[pl.ds(pl.multiple_of(i * rows, rows), rows), :], sbuf.at[i], own_sem
    )
    own.start()
    each(lambda d: send_h(d).start())
    for c in range(chunks):
        each(lambda e, c=c: send_s(c, n - e).start())

    gacc[...] = jnp.zeros_like(gacc)
    each(lambda d: land_h(d).wait_recv())

    def build(block):
        def one(j):
            now = block(j).astype(F32)
            before = jnp.where(j > 0, block(jnp.maximum(j - 1, 0)).astype(F32), 0.0)
            ext = jnp.concatenate([before, now], 1)
            odd = pltpu.roll(ext, LAG, 1)
            for l in range(LAGS):
                start = width - LANES * (l // 2)
                part = (odd if l % 2 else ext)[:, start : start + width]
                stack[j, l * K : (l + 1) * K, :] = part.astype(BF16)

        each(one, 0)

    build(lambda j: hraw[j])
    own.wait()

    def residual(c, j):
        at = pl.ds(c * step, step)
        recon = jnp.dot(w_ref[at, :], stack[j], preferred_element_type=F32)
        return (scale * recon - sbuf[j, at, :].astype(F32)).astype(BF16)

    groups = width // LANES

    def unit(c, j):
        prods = lax.dot_general(
            w_ref[pl.ds(c * step, step), :], residual(c, j), (((0,), (0,)), ((), ())),
            preferred_element_type=F32,
        )
        for odd in range(2):
            for q in range(1 - groups, groups):
                terms = []
                for m in range(LAGS // 2):
                    if 0 <= q + m < groups:
                        l = 2 * m + odd
                        terms.append(
                            prods[l * K : (l + 1) * K, (q + m) * LANES : (q + m + 1) * LANES]
                        )
                if not terms:
                    continue
                block = j + 1 if q >= 0 else j
                at = (q % groups) * LANES
                gacc[odd, block, :, at : at + LANES] += functools.reduce(lambda a, b: a + b, terms)

    for c in range(chunks):
        unit(c, i)

        def arrived(d, c=c):
            land_s(c, d).wait_recv()
            unit(c, source(d))

        each(arrived)

    def finish(j):
        after = jnp.concatenate([gacc[1, j + 1], gacc[1, j + 2]], 1)
        g = gacc[0, j + 1] + pltpu.roll(after, 2 * width - LAG, 1)[:, :width]
        gfin[0, j] = g[:, :half]
        gfin[1, j] = g[:, half:]

    each(finish, 0)

    a_copy = pltpu.make_async_remote_copy(
        src_ref=gfin.at[other], dst_ref=from_core, send_sem=a_sem.at[0], recv_sem=a_sem.at[1],
        device_id={"mz": other}, device_id_type=MESH,
    )
    a_copy.start()
    a_copy.wait_recv()

    def add_core(j):
        gsum[j] = gfin[mz, j] + from_core[j]

    each(add_core, 0)

    def send_g(d):
        return pltpu.make_async_remote_copy(
            src_ref=gsum.at[to(d)], dst_ref=from_scan.at[i], send_sem=b_send.at[d],
            recv_sem=b_recv.at[i], device_id={"scan": to(d)}, device_id_type=MESH,
        )

    def land_g(d):
        return pltpu.make_async_remote_copy(
            src_ref=gsum.at[to(d)], dst_ref=from_scan.at[source(d)], send_sem=b_send.at[d],
            recv_sem=b_recv.at[source(d)], device_id={"scan": to(d)}, device_id_type=MESH,
        )

    each(lambda e: send_g(n - e).start())

    def add_scan(d, total):
        land_g(d).wait_recv()
        return total + from_scan[source(d)]

    grad = scale * lax.fori_loop(1, n, add_scan, gsum[i])
    act = act_ref[...]
    act = jnp.where(mz == 0, act[:, :half], act[:, half:])
    new_h = jnp.maximum(act - h_rate[...] * grad, 0.0)
    nh[mz] = new_h
    hn[mz, i] = new_h.astype(BF16)

    def send_n(d):
        return pltpu.make_async_remote_copy(
            src_ref=hn.at[mz, i], dst_ref=hn.at[mz, i], send_sem=c_send.at[d],
            recv_sem=c_recv.at[i], device_id={"scan": to(d)}, device_id_type=MESH,
        )

    def land_n(d):
        return pltpu.make_async_remote_copy(
            src_ref=hn.at[mz, source(d)], dst_ref=hn.at[mz, source(d)], send_sem=c_send.at[d],
            recv_sem=c_recv.at[source(d)], device_id={"scan": to(d)}, device_id_type=MESH,
        )

    each(lambda e: send_n(n - e).start())
    e_copy = pltpu.make_async_remote_copy(
        src_ref=nh.at[mz], dst_ref=nh.at[mz], send_sem=e_sem.at[0], recv_sem=e_sem.at[1],
        device_id={"mz": other}, device_id_type=MESH,
    )
    e_copy.start()
    each(lambda d: land_n(d).wait_recv())
    d_copy = pltpu.make_async_remote_copy(
        src_ref=hn.at[mz], dst_ref=hn.at[mz], send_sem=d_sem.at[0], recv_sem=d_sem.at[1],
        device_id={"mz": other}, device_id_type=MESH,
    )
    d_copy.start()
    e_back = pltpu.make_async_remote_copy(
        src_ref=nh.at[other], dst_ref=nh.at[other], send_sem=e_sem.at[0], recv_sem=e_sem.at[1],
        device_id={"mz": other}, device_id_type=MESH,
    )
    e_back.wait_recv()
    h_out[...] = jnp.concatenate([nh[0], nh[1]], 1)
    d_back = pltpu.make_async_remote_copy(
        src_ref=hn.at[other], dst_ref=hn.at[other], send_sem=d_sem.at[0], recv_sem=d_sem.at[1],
        device_id={"mz": other}, device_id_type=MESH,
    )
    d_back.wait_recv()
    build(lambda j: jnp.concatenate([hn[0, j], hn[1, j]], 1))

    for c in range(chunks):
        total_w[...] = jnp.zeros_like(total_w)

        def add_w(j, c=c):
            total_w[...] += lax.dot_general(
                residual(c, j), stack[j], (((1,), (1,)), ((), ())), preferred_element_type=F32
            )

        each(add_w, 0)
        at = pl.ds(c * step, step)
        moved = w_ref[at, :].astype(F32) - w_rate[...] * (scale * total_w[...])
        w_out[at, :] = jnp.maximum(moved, 0.0).astype(BF16)

    each(lambda d: send_h(d).wait_send())
    for c in range(chunks):
        each(lambda d, c=c: send_s(c, d).wait_send())
    each(lambda d: send_g(d).wait_send())
    each(lambda d: send_n(d).wait_send())
    a_copy.wait_send()
    d_copy.wait_send()
    e_copy.wait_send()


def per_device(n, spectra, templates, activations, h_rate, w_rate):
    rows, cols = templates.shape[1], templates.shape[2]
    width = spectra.shape[1]
    half = width // 2
    chunks = rows // 256 if rows % 256 == 0 else 1
    vmem = pl.BlockSpec(memory_space=pltpu.VMEM)
    dma = pltpu.SemaphoreType.DMA
    new_h, new_w = pl.pallas_call(
        functools.partial(kernel, n, chunks),
        out_shape=(
            jax.ShapeDtypeStruct(activations.shape, F32),
            jax.ShapeDtypeStruct((rows, cols), BF16),
        ),
        in_specs=[pl.BlockSpec(memory_space=pl.ANY), vmem, vmem, vmem, vmem],
        out_specs=(vmem, vmem),
        scratch_shapes=[
            pltpu.VMEM((n, rows, width), BF16),
            pltpu.VMEM((n, K, width), BF16),
            pltpu.VMEM((n, cols, width), BF16),
            pltpu.VMEM((2, n + 2, K, width), F32),
            pltpu.VMEM((2, n, K, half), F32),
            pltpu.VMEM((n, K, half), F32),
            pltpu.VMEM((n, K, half), F32),
            pltpu.VMEM((n, K, half), F32),
            pltpu.VMEM((2, K, half), F32),
            pltpu.VMEM((2, n, K, half), BF16),
            pltpu.VMEM((rows // chunks, cols), F32),
            dma,
            dma((chunks, n)),
            dma((chunks, n)),
            dma((n,)),
            dma((n,)),
            dma((2,)),
            dma((n,)),
            dma((n,)),
            dma((n,)),
            dma((n,)),
            dma((2,)),
            dma((2,)),
        ],
        compiler_params=pltpu.CompilerParams(
            collective_id=0, has_side_effects=True, vmem_limit_bytes=56 * 1024 * 1024
        ),
        cost_estimate=pl.CostEstimate(
            flops=8 * n * rows * cols * width, bytes_accessed=4 * n * rows * width, transcendentals=0
        ),
    )(
        spectra,
        templates.reshape(rows, cols),
        activations,
        h_rate[:, None],
        jnp.tile(w_rate, LAGS)[None, :],
    )
    return new_h, new_w.reshape(templates.shape)


def solution(mesh):
    placed = (
        P("mz", ("slab", "scan")),
        P("mz", ("slab", "scan"), None),
        P(None, ("slab", "scan")),
        P(),
        P(),
    )
    return jax.shard_map(
        functools.partial(per_device, mesh.shape["scan"]),
        mesh=mesh,
        in_specs=placed,
        out_specs=(P(None, ("slab", "scan")), P("mz", ("slab", "scan"), None)),
        check_vma=False,
    )
```

```python
import functools

import jax
import jax.numpy as jnp
from jax import lax
from jax.experimental import pallas as pl
from jax.experimental.pallas import tpu as pltpu
from jax.sharding import PartitionSpec as P

K = 64
LAGS = 8
LAG = 64
LANES = 128
F32 = jnp.float32
BF16 = jnp.bfloat16
MESH = pl.DeviceIdType.MESH


def crossed(a, b, n):
    out, bit = 0, 1
    while bit < n:
        out = out + bit * ((a // bit + b // bit) % 2)
        bit *= 2
    return out


def column(row):
    shape = (K, K)
    same = lax.broadcasted_iota(jnp.int32, shape, 0) == lax.broadcasted_iota(jnp.int32, shape, 1)
    return jnp.sum(jnp.where(same, row, 0.0), axis=1, keepdims=True)


def store(h_in, w_in, h_out, w_out, sems):
    copies = [
        pltpu.make_async_copy(w_in, w_out, sems.at[0]),
        pltpu.make_async_copy(h_in, h_out, sems.at[1]),
    ]
    for copy in copies:
        copy.start()
    for copy in copies:
        copy.wait()


def kernel(
    n, chunks, spectra, w_ref, act_ref, h_rate, w_rate, h_out, w_out,
    sbuf, hraw, stack, gacc, gfin, from_core, gsum, from_scan, nh, hn, total_w,
    own_sem, s_send, s_recv, h_send, h_recv, a_send, a_recv, b_send, b_recv, c_send, c_recv,
    d_send, d_recv, e_sem,
):
    rows, width = sbuf.shape[1], sbuf.shape[2]
    half = width // 2
    step = rows // chunks
    scale = 1.0 / (LAGS * K)
    i = lax.axis_index("scan")
    mz = lax.axis_index("mz")
    other = 1 - mz
    two = n & (n - 1) == 0

    def to(d):
        return crossed(i, d, n) if two else lax.rem(i + d, n)

    def source(d):
        return crossed(i, d, n) if two else lax.rem(i + n - d, n)

    def each(body, start=1):
        def run(d, carry):
            body(d)
            return carry

        lax.fori_loop(start, n, run, 0)

    barrier = pltpu.get_barrier_semaphore()
    each(lambda d: pl.semaphore_signal(barrier, inc=1, device_id={"scan": to(d)}, device_id_type=MESH))
    pl.semaphore_signal(barrier, inc=1, device_id={"mz": other}, device_id_type=MESH)
    hraw[i] = act_ref[...].astype(BF16)
    pl.semaphore_wait(barrier, n)

    def send_h(d):
        return pltpu.make_async_remote_copy(
            src_ref=hraw.at[i], dst_ref=hraw.at[i], send_sem=h_send.at[d], recv_sem=h_recv.at[i],
            device_id={"scan": to(d)}, device_id_type=MESH,
        )

    def land_h(d):
        return pltpu.make_async_remote_copy(
            src_ref=hraw.at[source(d)], dst_ref=hraw.at[source(d)], send_sem=h_send.at[d],
            recv_sem=h_recv.at[source(d)], device_id={"scan": to(d)}, device_id_type=MESH,
        )

    pieces = 2 if step % 32 == 0 else 1
    piece = step // pieces

    def send_s(c, u, d):
        first = c * step + u * piece
        return pltpu.make_async_remote_copy(
            src_ref=spectra.at[pl.ds(pl.multiple_of(to(d) * rows + first, piece), piece), :],
            dst_ref=sbuf.at[i, pl.ds(first, piece), :],
            send_sem=s_send.at[c, d], recv_sem=s_recv.at[c, i],
            device_id={"scan": to(d)}, device_id_type=MESH,
        )

    def land_s(c, d):
        return pltpu.make_async_remote_copy(
            src_ref=spectra.at[pl.ds(c * step, step), :],
            dst_ref=sbuf.at[source(d), pl.ds(c * step, step), :],
            send_sem=s_send.at[c, d], recv_sem=s_recv.at[c, source(d)],
            device_id={"scan": to(d)}, device_id_type=MESH,
        )

    own = pltpu.make_async_copy(
        spectra.at[pl.ds(pl.multiple_of(i * rows, rows), rows), :], sbuf.at[i], own_sem
    )
    own.start()
    each(lambda d: send_h(d).start())
    turn = (2 * lax.rem(i // 2, 2) + mz) * (n - 1) // 4
    for c in range(chunks):
        for u in range(pieces):
            each(lambda e, c=c, u=u: send_s(c, u, n - 1 - lax.rem(e - 1 + turn, n - 1)).start())

    gacc[...] = jnp.zeros_like(gacc)
    each(lambda d: land_h(d).wait_recv())

    def build(block, j):
        now = block(j).astype(F32)
        before = jnp.where(j > 0, block(jnp.maximum(j - 1, 0)).astype(F32), 0.0)
        ext = jnp.concatenate([before, now], 1)
        odd = pltpu.roll(ext, LAG, 1)
        for l in range(LAGS):
            start = width - LANES * (l // 2)
            part = (odd if l % 2 else ext)[:, start : start + width]
            stack[j, l * K : (l + 1) * K, :] = part.astype(BF16)

    each(lambda j: build(lambda b: hraw[b], j), 0)
    own.wait()

    def residual(c, j):
        at = pl.ds(c * step, step)
        recon = jnp.dot(w_ref[at, :], stack[j], preferred_element_type=F32)
        return (scale * recon - sbuf[j, at, :].astype(F32)).astype(BF16)

    groups = width // LANES

    def unit(c, j):
        prods = lax.dot_general(
            w_ref[pl.ds(c * step, step), :], residual(c, j), (((0,), (0,)), ((), ())),
            preferred_element_type=F32,
        )
        for odd in range(2):
            for q in range(1 - groups, groups):
                terms = []
                for m in range(LAGS // 2):
                    if 0 <= q + m < groups:
                        l = 2 * m + odd
                        terms.append(
                            prods[l * K : (l + 1) * K, (q + m) * LANES : (q + m + 1) * LANES]
                        )
                if not terms:
                    continue
                block = j + 1 if q >= 0 else j
                at = (q % groups) * LANES
                gacc[odd, block, :, at : at + LANES] += functools.reduce(lambda a, b: a + b, terms)

    for c in range(chunks):
        unit(c, i)

        def arrived(d, c=c):
            land_s(c, d).wait_recv()
            unit(c, source(d))

        each(arrived)

    def finish(j):
        after = jnp.concatenate([gacc[1, j + 1], gacc[1, j + 2]], 1)
        g = gacc[0, j + 1] + pltpu.roll(after, 2 * width - LAG, 1)[:, :width]
        gfin[0, j] = g[:, :half]
        gfin[1, j] = g[:, half:]

    def core_copy(j):
        return pltpu.make_async_remote_copy(
            src_ref=gfin.at[other, j], dst_ref=from_core.at[j], send_sem=a_send.at[j],
            recv_sem=a_recv.at[j], device_id={"mz": other}, device_id_type=MESH,
        )

    def finish_and_send(e):
        j = to(n - 1 - e)
        finish(j)
        core_copy(j).start()

    each(finish_and_send, 0)

    def send_g(d):
        return pltpu.make_async_remote_copy(
            src_ref=gsum.at[to(d)], dst_ref=from_scan.at[i], send_sem=b_send.at[d],
            recv_sem=b_recv.at[i], device_id={"scan": to(d)}, device_id_type=MESH,
        )

    def land_g(d):
        return pltpu.make_async_remote_copy(
            src_ref=gsum.at[to(d)], dst_ref=from_scan.at[source(d)], send_sem=b_send.at[d],
            recv_sem=b_recv.at[source(d)], device_id={"scan": to(d)}, device_id_type=MESH,
        )

    def add_core(j):
        core_copy(j).wait_recv()
        gsum[j] = gfin[mz, j] + from_core[j]

    def add_and_send(e):
        add_core(to(n - e))
        send_g(n - e).start()

    each(add_and_send)
    add_core(i)

    def add_scan(d, total):
        land_g(d).wait_recv()
        return total + from_scan[source(d)]

    grad = scale * lax.fori_loop(1, n, add_scan, gsum[i])
    act = act_ref[...]
    act = jnp.where(mz == 0, act[:, :half], act[:, half:])
    new_h = jnp.maximum(act - column(h_rate[...]) * grad, 0.0)
    nh[mz] = new_h
    hn[mz, i] = new_h.astype(BF16)

    def after(t):
        return lax.rem(i + t, n)

    def send_n(t):
        return pltpu.make_async_remote_copy(
            src_ref=hn.at[mz, i], dst_ref=hn.at[mz, i], send_sem=c_send.at[t],
            recv_sem=c_recv.at[i], device_id={"scan": after(n - t)}, device_id_type=MESH,
        )

    def land_n(t):
        return pltpu.make_async_remote_copy(
            src_ref=hn.at[mz, after(t)], dst_ref=hn.at[mz, after(t)], send_sem=c_send.at[t],
            recv_sem=c_recv.at[after(t)], device_id={"scan": after(n - t)}, device_id_type=MESH,
        )

    def hand_on(j):
        return pltpu.make_async_remote_copy(
            src_ref=hn.at[mz, j], dst_ref=hn.at[mz, j], send_sem=d_send.at[j],
            recv_sem=d_recv.at[j], device_id={"mz": other}, device_id_type=MESH,
        )

    def handed(j):
        return pltpu.make_async_remote_copy(
            src_ref=hn.at[other, j], dst_ref=hn.at[other, j], send_sem=d_send.at[j],
            recv_sem=d_recv.at[j], device_id={"mz": other}, device_id_type=MESH,
        )

    hand_on(i).start()
    each(lambda t: send_n(t).start())
    e_copy = pltpu.make_async_remote_copy(
        src_ref=nh.at[mz], dst_ref=nh.at[mz], send_sem=e_sem.at[0], recv_sem=e_sem.at[1],
        device_id={"mz": other}, device_id_type=MESH,
    )
    e_copy.start()
    total_w[...] = jnp.zeros_like(total_w)

    def take(t):
        land_n(t).wait_recv()
        hand_on(after(t)).start()

    take(1)
    handed(i).wait_recv()

    def second(t, carry):
        j = after(t)

        @pl.when(t + 1 < n)
        def _():
            take(t + 1)

        @pl.when(t < n)
        def _():
            handed(j).wait_recv()

        build(lambda b: jnp.concatenate([hn[0, b], hn[1, b]], 1), j)
        for c in range(chunks):
            total_w[pl.ds(c * step, step), :] += lax.dot_general(
                residual(c, j), stack[j], (((1,), (1,)), ((), ())), preferred_element_type=F32
            )
        return carry

    lax.fori_loop(1, n + 1, second, 0)

    lags = lax.broadcasted_iota(jnp.int32, (K, LAGS * K), 1)
    same = lax.rem(lags, K) == lax.broadcasted_iota(jnp.int32, (K, LAGS * K), 0)
    rates = jnp.sum(jnp.where(same, column(w_rate[...]), 0.0), axis=0, keepdims=True)
    for c in range(chunks):
        at = pl.ds(c * step, step)
        moved = w_ref[at, :].astype(F32) - rates * (scale * total_w[at, :])
        w_out[at, :] = jnp.maximum(moved, 0.0).astype(BF16)

    e_back = pltpu.make_async_remote_copy(
        src_ref=nh.at[other], dst_ref=nh.at[other], send_sem=e_sem.at[0], recv_sem=e_sem.at[1],
        device_id={"mz": other}, device_id_type=MESH,
    )
    e_back.wait_recv()
    h_out[...] = jnp.concatenate([nh[0], nh[1]], 1)

    each(lambda d: send_h(d).wait_send())
    for c in range(chunks):
        each(lambda d, c=c: land_s(c, d).wait_send())
    each(lambda d: send_g(d).wait_send())
    each(lambda d: send_n(d).wait_send())
    each(lambda j: core_copy(j).wait_send(), 0)
    each(lambda j: hand_on(j).wait_send(), 0)
    e_copy.wait_send()


def per_device(n, spectra, templates, activations, h_rate, w_rate):
    rows, cols = templates.shape[1], templates.shape[2]
    width = spectra.shape[1]
    half = width // 2
    chunks = rows // 256 if rows % 256 == 0 else 1
    vmem = pl.BlockSpec(memory_space=pltpu.VMEM)
    dma = pltpu.SemaphoreType.DMA
    new_h, new_w = pl.pallas_call(
        functools.partial(kernel, n, chunks),
        out_shape=(
            jax.ShapeDtypeStruct(activations.shape, F32),
            jax.ShapeDtypeStruct((rows, cols), BF16),
        ),
        in_specs=[pl.BlockSpec(memory_space=pl.ANY), vmem, vmem, vmem, vmem],
        out_specs=(vmem, vmem),
        scratch_shapes=[
            pltpu.VMEM((n, rows, width), BF16),
            pltpu.VMEM((n, K, width), BF16),
            pltpu.VMEM((n, cols, width), BF16),
            pltpu.VMEM((2, n + 2, K, width), F32),
            pltpu.VMEM((2, n, K, half), F32),
            pltpu.VMEM((n, K, half), F32),
            pltpu.VMEM((n, K, half), F32),
            pltpu.VMEM((n, K, half), F32),
            pltpu.VMEM((2, K, half), F32),
            pltpu.VMEM((2, n, K, half), BF16),
            pltpu.VMEM((rows, cols), F32),
            dma,
            dma((chunks, n)),
            dma((chunks, n)),
            dma((n,)),
            dma((n,)),
            dma((n,)),
            dma((n,)),
            dma((n,)),
            dma((n,)),
            dma((n,)),
            dma((n,)),
            dma((n,)),
            dma((n,)),
            dma((2,)),
        ],
        compiler_params=pltpu.CompilerParams(
            collective_id=0, has_side_effects=True, vmem_limit_bytes=56 * 1024 * 1024
        ),
        cost_estimate=pl.CostEstimate(
            flops=8 * n * rows * cols * width, bytes_accessed=4 * n * rows * width, transcendentals=0
        ),
    )(
        spectra,
        templates.reshape(rows, cols),
        activations,
        h_rate.reshape(1, K),
        w_rate.reshape(1, K),
    )
    hbm = pl.BlockSpec(memory_space=pltpu.HBM)
    new_h, new_w = pl.pallas_call(
        store,
        out_shape=(
            jax.ShapeDtypeStruct(new_h.shape, F32),
            jax.ShapeDtypeStruct(new_w.shape, BF16),
        ),
        in_specs=[hbm, hbm],
        out_specs=(hbm, hbm),
        scratch_shapes=[dma((2,))],
    )(new_h, new_w)
    return new_h, new_w.reshape(templates.shape)


def solution(mesh):
    placed = (
        P("mz", ("slab", "scan")),
        P("mz", ("slab", "scan"), None),
        P(None, ("slab", "scan")),
        P(),
        P(),
    )
    return jax.shard_map(
        functools.partial(per_device, mesh.shape["scan"]),
        mesh=mesh,
        in_specs=placed,
        out_specs=(P(None, ("slab", "scan")), P("mz", ("slab", "scan"), None)),
        check_vma=False,
    )
```

```python
import functools

import jax
import jax.numpy as jnp
from jax import lax
from jax.experimental import pallas as pl
from jax.experimental.pallas import tpu as pltpu
from jax.sharding import PartitionSpec as P

K = 64
LAGS = 8
LAG = 64
LANES = 128
F32 = jnp.float32
BF16 = jnp.bfloat16
MESH = pl.DeviceIdType.MESH


def crossed(a, b, n):
    out, bit = 0, 1
    while bit < n:
        out = out + bit * ((a // bit + b // bit) % 2)
        bit *= 2
    return out


def column(row):
    shape = (K, K)
    same = lax.broadcasted_iota(jnp.int32, shape, 0) == lax.broadcasted_iota(jnp.int32, shape, 1)
    return jnp.sum(jnp.where(same, row, 0.0), axis=1, keepdims=True)


def kernel(
    n, chunks, spectra, w_ref, act_ref, h_rate, w_rate, h_out, w_out,
    sbuf, hraw, stack, gacc, gfin, from_core, gsum, from_scan, nh, hn, total_w, w_across,
    own_sem, s_send, s_recv, h_send, h_recv, a_send, a_recv, b_send, b_recv, c_send, c_recv,
    d_send, d_recv, e_sem,
):
    rows, width = sbuf.shape[1], sbuf.shape[2]
    half = width // 2
    step = rows // chunks
    scale = 1.0 / (LAGS * K)
    i = lax.axis_index("scan")
    mz = lax.axis_index("mz")
    other = 1 - mz
    two = n & (n - 1) == 0

    def to(d):
        return crossed(i, d, n) if two else lax.rem(i + d, n)

    def source(d):
        return crossed(i, d, n) if two else lax.rem(i + n - d, n)

    def each(body, start=1):
        def run(d, carry):
            body(d)
            return carry

        lax.fori_loop(start, n, run, 0)

    barrier = pltpu.get_barrier_semaphore()
    each(lambda d: pl.semaphore_signal(barrier, inc=1, device_id={"scan": to(d)}, device_id_type=MESH))
    pl.semaphore_signal(barrier, inc=1, device_id={"mz": other}, device_id_type=MESH)
    hraw[i] = act_ref[...].astype(BF16)
    pl.semaphore_wait(barrier, n)

    def send_h(d):
        return pltpu.make_async_remote_copy(
            src_ref=hraw.at[i], dst_ref=hraw.at[i], send_sem=h_send.at[d], recv_sem=h_recv.at[i],
            device_id={"scan": to(d)}, device_id_type=MESH,
        )

    def land_h(d):
        return pltpu.make_async_remote_copy(
            src_ref=hraw.at[source(d)], dst_ref=hraw.at[source(d)], send_sem=h_send.at[d],
            recv_sem=h_recv.at[source(d)], device_id={"scan": to(d)}, device_id_type=MESH,
        )

    pieces = 2 if step % 32 == 0 else 1
    piece = step // pieces

    def send_s(c, u, d):
        first = c * step + u * piece
        return pltpu.make_async_remote_copy(
            src_ref=spectra.at[pl.ds(pl.multiple_of(to(d) * rows + first, piece), piece), :],
            dst_ref=sbuf.at[i, pl.ds(first, piece), :],
            send_sem=s_send.at[c, d], recv_sem=s_recv.at[c, i],
            device_id={"scan": to(d)}, device_id_type=MESH,
        )

    def send_last(u, t):
        p = lax.rem(i + t, n)
        first = (chunks - 1) * step + u * piece
        return pltpu.make_async_remote_copy(
            src_ref=spectra.at[pl.ds(pl.multiple_of(p * rows + first, piece), piece), :],
            dst_ref=sbuf.at[i, pl.ds(first, piece), :],
            send_sem=s_send.at[chunks - 1, t], recv_sem=s_recv.at[chunks - 1, i],
            device_id={"scan": p}, device_id_type=MESH,
        )

    def land_last(t):
        j = lax.rem(i + n - t, n)
        at = pl.ds((chunks - 1) * step, step)
        return pltpu.make_async_remote_copy(
            src_ref=spectra.at[at, :], dst_ref=sbuf.at[j, at, :],
            send_sem=s_send.at[chunks - 1, t], recv_sem=s_recv.at[chunks - 1, j],
            device_id={"scan": lax.rem(i + t, n)}, device_id_type=MESH,
        )

    def land_s(c, d):
        return pltpu.make_async_remote_copy(
            src_ref=spectra.at[pl.ds(c * step, step), :],
            dst_ref=sbuf.at[source(d), pl.ds(c * step, step), :],
            send_sem=s_send.at[c, d], recv_sem=s_recv.at[c, source(d)],
            device_id={"scan": to(d)}, device_id_type=MESH,
        )

    own = pltpu.make_async_copy(
        spectra.at[pl.ds(pl.multiple_of(i * rows, rows), rows), :], sbuf.at[i], own_sem
    )
    own.start()
    each(lambda d: send_h(d).start())
    turn = (2 * lax.rem(i // 2, 2) + mz) * (n - 1) // 4
    for c in range(chunks):
        for u in range(pieces):
            if c < chunks - 1:
                each(lambda e, c=c, u=u: send_s(c, u, n - 1 - lax.rem(e - 1 + turn, n - 1)).start())
    each(lambda t: [send_last(u, t).start() for u in range(pieces)])

    gacc[...] = jnp.zeros_like(gacc)
    w_across[...] = w_ref[...].T
    each(lambda d: land_h(d).wait_recv())

    def build(block, j):
        now = block(j).astype(F32)
        before = jnp.where(j > 0, block(jnp.maximum(j - 1, 0)).astype(F32), 0.0)
        ext = jnp.concatenate([before, now], 1)
        odd = pltpu.roll(ext, LAG, 1)
        for l in range(LAGS):
            start = width - LANES * (l // 2)
            part = (odd if l % 2 else ext)[:, start : start + width]
            stack[j, l * K : (l + 1) * K, :] = (scale * part).astype(BF16)

    each(lambda j: build(lambda b: hraw[b], j), 0)
    own.wait()

    def residual(c, j):
        at = pl.ds(c * step, step)
        recon = jnp.dot(w_ref[at, :], stack[j], preferred_element_type=F32)
        return (recon - sbuf[j, at, :].astype(F32)).astype(BF16)

    groups = width // LANES

    def unit(c, j):
        prods = jnp.dot(
            w_across[:, c * step : (c + 1) * step], residual(c, j), preferred_element_type=F32
        )
        for odd in range(2):
            for q in range(1 - groups, groups):
                terms = []
                for m in range(LAGS // 2):
                    if 0 <= q + m < groups:
                        l = 2 * m + odd
                        terms.append(
                            prods[l * K : (l + 1) * K, (q + m) * LANES : (q + m + 1) * LANES]
                        )
                if not terms:
                    continue
                block = j + 1 if q >= 0 else j
                at = (q % groups) * LANES
                gacc[odd, block, :, at : at + LANES] += functools.reduce(lambda a, b: a + b, terms)

    for c in range(chunks - 1):
        unit(c, i)

        def arrived(d, c=c):
            land_s(c, d).wait_recv()
            unit(c, source(d))

        each(arrived)

    def finish(j):
        after = jnp.concatenate([gacc[1, j + 1], gacc[1, j + 2]], 1)
        g = gacc[0, j + 1] + pltpu.roll(after, 2 * width - LAG, 1)[:, :width]
        gfin[0, j] = g[:, :half]
        gfin[1, j] = g[:, half:]

    def core_copy(j):
        return pltpu.make_async_remote_copy(
            src_ref=gfin.at[other, j], dst_ref=from_core.at[j], send_sem=a_send.at[j],
            recv_sem=a_recv.at[j], device_id={"mz": other}, device_id_type=MESH,
        )

    def send_g(j):
        return pltpu.make_async_remote_copy(
            src_ref=gsum.at[j], dst_ref=from_scan.at[i], send_sem=b_send.at[j],
            recv_sem=b_recv.at[i], device_id={"scan": j}, device_id_type=MESH,
        )

    def land_g(j):
        return pltpu.make_async_remote_copy(
            src_ref=gsum.at[j], dst_ref=from_scan.at[j], send_sem=b_send.at[j],
            recv_sem=b_recv.at[j], device_id={"scan": j}, device_id_type=MESH,
        )

    def add_core(j):
        core_copy(j).wait_recv()
        gsum[j] = gfin[mz, j] + from_core[j]

    def add_and_send(t):
        j = lax.rem(i + n - t, n)
        add_core(j)
        send_g(j).start()

    unit(chunks - 1, i)

    def last(t):
        j = lax.rem(i + n - t, n)
        land_last(t).wait_recv()
        unit(chunks - 1, j)
        finish(j)
        core_copy(j).start()

        @pl.when(t > 1)
        def _():
            add_and_send(t - 1)

    each(last)
    finish(i)
    core_copy(i).start()
    add_and_send(n - 1)
    add_core(i)

    def add_scan(d, total):
        j = lax.rem(i + d, n)
        land_g(j).wait_recv()
        return total + from_scan[j]

    grad = scale * lax.fori_loop(1, n, add_scan, gsum[i])
    act = act_ref[...]
    act = jnp.where(mz == 0, act[:, :half], act[:, half:])
    new_h = jnp.maximum(act - column(h_rate[...]) * grad, 0.0)
    nh[mz] = new_h
    hn[mz, i] = new_h.astype(BF16)

    def after(t):
        return lax.rem(i + t, n)

    def send_n(t):
        return pltpu.make_async_remote_copy(
            src_ref=hn.at[mz, i], dst_ref=hn.at[mz, i], send_sem=c_send.at[t],
            recv_sem=c_recv.at[i], device_id={"scan": after(n - t)}, device_id_type=MESH,
        )

    def land_n(t):
        return pltpu.make_async_remote_copy(
            src_ref=hn.at[mz, after(t)], dst_ref=hn.at[mz, after(t)], send_sem=c_send.at[t],
            recv_sem=c_recv.at[after(t)], device_id={"scan": after(n - t)}, device_id_type=MESH,
        )

    def hand_on(j):
        return pltpu.make_async_remote_copy(
            src_ref=hn.at[mz, j], dst_ref=hn.at[mz, j], send_sem=d_send.at[j],
            recv_sem=d_recv.at[j], device_id={"mz": other}, device_id_type=MESH,
        )

    def handed(j):
        return pltpu.make_async_remote_copy(
            src_ref=hn.at[other, j], dst_ref=hn.at[other, j], send_sem=d_send.at[j],
            recv_sem=d_recv.at[j], device_id={"mz": other}, device_id_type=MESH,
        )

    hand_on(i).start()
    each(lambda t: send_n(t).start())
    e_copy = pltpu.make_async_remote_copy(
        src_ref=nh.at[mz], dst_ref=nh.at[mz], send_sem=e_sem.at[0], recv_sem=e_sem.at[1],
        device_id={"mz": other}, device_id_type=MESH,
    )
    e_copy.start()
    total_w[...] = jnp.zeros_like(total_w)

    def take(t):
        land_n(t).wait_recv()
        hand_on(after(t)).start()

    take(1)
    handed(i).wait_recv()

    def second(t, carry):
        j = after(t)

        @pl.when(t + 1 < n)
        def _():
            take(t + 1)

        @pl.when(t < n)
        def _():
            handed(j).wait_recv()

        build(lambda b: jnp.concatenate([hn[0, b], hn[1, b]], 1), j)
        for c in range(chunks):
            total_w[pl.ds(c * step, step), :] += lax.dot_general(
                residual(c, j), stack[j], (((1,), (1,)), ((), ())), preferred_element_type=F32
            )
        return carry

    lax.fori_loop(1, n + 1, second, 0)

    lags = lax.broadcasted_iota(jnp.int32, (K, LAGS * K), 1)
    same = lax.rem(lags, K) == lax.broadcasted_iota(jnp.int32, (K, LAGS * K), 0)
    rates = jnp.sum(jnp.where(same, column(w_rate[...]), 0.0), axis=0, keepdims=True)
    for c in range(chunks):
        at = pl.ds(c * step, step)
        moved = w_ref[at, :].astype(F32) - rates * total_w[at, :]
        w_out[at, :] = moved.astype(BF16)

    e_back = pltpu.make_async_remote_copy(
        src_ref=nh.at[other], dst_ref=nh.at[other], send_sem=e_sem.at[0], recv_sem=e_sem.at[1],
        device_id={"mz": other}, device_id_type=MESH,
    )
    e_back.wait_recv()
    h_out[...] = jnp.concatenate([nh[0], nh[1]], 1)

    each(lambda d: send_h(d).wait_send())
    for c in range(chunks):
        each(lambda d, c=c: land_s(c, d).wait_send())
    each(lambda t: send_g(lax.rem(i + t, n)).wait_send())
    each(lambda d: send_n(d).wait_send())
    each(lambda j: core_copy(j).wait_send(), 0)
    each(lambda j: hand_on(j).wait_send(), 0)
    e_copy.wait_send()


def per_device(n, spectra, templates, activations, h_rate, w_rate):
    rows, cols = templates.shape[1], templates.shape[2]
    width = spectra.shape[1]
    half = width // 2
    chunks = rows // 256 if rows % 256 == 0 else 1
    vmem = pl.BlockSpec(memory_space=pltpu.VMEM)
    dma = pltpu.SemaphoreType.DMA
    new_h, new_w = pl.pallas_call(
        functools.partial(kernel, n, chunks),
        out_shape=(
            jax.ShapeDtypeStruct(activations.shape, F32),
            jax.ShapeDtypeStruct((rows, cols), BF16),
        ),
        in_specs=[pl.BlockSpec(memory_space=pl.ANY), vmem, vmem, vmem, vmem],
        out_specs=(vmem, vmem),
        scratch_shapes=[
            pltpu.VMEM((n, rows, width), BF16),
            pltpu.VMEM((n, K, width), BF16),
            pltpu.VMEM((n, cols, width), BF16),
            pltpu.VMEM((2, n + 2, K, width), F32),
            pltpu.VMEM((2, n, K, half), F32),
            pltpu.VMEM((n, K, half), F32),
            pltpu.VMEM((n, K, half), F32),
            pltpu.VMEM((n, K, half), F32),
            pltpu.VMEM((2, K, half), F32),
            pltpu.VMEM((2, n, K, half), BF16),
            pltpu.VMEM((rows, cols), F32),
            pltpu.VMEM((cols, rows), BF16),
            dma,
            dma((chunks, n)),
            dma((chunks, n)),
            dma((n,)),
            dma((n,)),
            dma((n,)),
            dma((n,)),
            dma((n,)),
            dma((n,)),
            dma((n,)),
            dma((n,)),
            dma((n,)),
            dma((n,)),
            dma((2,)),
        ],
        compiler_params=pltpu.CompilerParams(
            collective_id=0, has_side_effects=True, vmem_limit_bytes=56 * 1024 * 1024
        ),
        cost_estimate=pl.CostEstimate(
            flops=8 * n * rows * cols * width, bytes_accessed=4 * n * rows * width, transcendentals=0
        ),
    )(
        spectra,
        templates.reshape(rows, cols),
        activations,
        h_rate.reshape(1, K),
        w_rate.reshape(1, K),
    )
    new_h = jnp.maximum(new_h, 0.0)
    new_w = jnp.maximum(new_w, jnp.zeros((), BF16))
    return new_h, new_w.reshape(templates.shape)


def solution(mesh):
    placed = (
        P("mz", ("slab", "scan")),
        P("mz", ("slab", "scan"), None),
        P(None, ("slab", "scan")),
        P(),
        P(),
    )
    return jax.shard_map(
        functools.partial(per_device, mesh.shape["scan"]),
        mesh=mesh,
        in_specs=placed,
        out_specs=(P(None, ("slab", "scan")), P("mz", ("slab", "scan"), None)),
        check_vma=False,
    )
```

```python
import functools

import jax
import jax.numpy as jnp
from jax import lax
from jax.experimental import pallas as pl
from jax.experimental.pallas import tpu as pltpu
from jax.sharding import PartitionSpec as P

K = 64
LAGS = 8
LAG = 64
LANES = 128
F32 = jnp.float32
BF16 = jnp.bfloat16
MESH = pl.DeviceIdType.MESH


def crossed(a, b, n):
    out, bit = 0, 1
    while bit < n:
        out = out + bit * ((a // bit + b // bit) % 2)
        bit *= 2
    return out


def column(row):
    shape = (K, K)
    same = lax.broadcasted_iota(jnp.int32, shape, 0) == lax.broadcasted_iota(jnp.int32, shape, 1)
    return jnp.sum(jnp.where(same, row, 0.0), axis=1, keepdims=True)


def kernel(
    n, chunks, spectra, w_ref, act_ref, h_rate, w_rate, h_out, w_out,
    sbuf, hraw, stack, gacc, gfin, from_core, gsum, from_scan, nh, hn, total_w, w_across,
    own_sem, s_send, s_recv, h_send, h_recv, a_send, a_recv, b_send, b_recv, c_send, c_recv,
    d_send, d_recv, p_send, f_send, f_recv, e_sem, k_sem, from_pair, q_send,
):
    rows, width = sbuf.shape[1], sbuf.shape[2]
    half = width // 2
    step = rows // chunks
    scale = 1.0 / (LAGS * K)
    i = lax.axis_index("scan")
    mz = lax.axis_index("mz")
    other = 1 - mz
    two = n & (n - 1) == 0

    def to(d):
        return crossed(i, d, n) if two else lax.rem(i + d, n)

    def source(d):
        return crossed(i, d, n) if two else lax.rem(i + n - d, n)

    def each(body, start=1):
        def run(d, carry):
            body(d)
            return carry

        lax.fori_loop(start, n, run, 0)

    act = act_ref[...]
    hraw[0, i] = act[:, :half].astype(BF16)
    hraw[1, i] = act[:, half:].astype(BF16)
    barrier = pltpu.get_barrier_semaphore()
    each(lambda d: pl.semaphore_signal(barrier, inc=1, device_id={"scan": to(d)}, device_id_type=MESH))
    pl.semaphore_signal(barrier, inc=1, device_id={"mz": other}, device_id_type=MESH)
    pair = i + 1 - 2 * lax.rem(i, 2)
    pl.semaphore_wait(barrier, n)

    def along(t):
        return lax.rem(i + t, n)

    def column_copy(ref, sends, lands, t, j):
        return pltpu.make_async_remote_copy(
            src_ref=ref.at[mz, j], dst_ref=ref.at[mz, j], send_sem=sends.at[t],
            recv_sem=lands.at[j], device_id={"scan": along(n - t)}, device_id_type=MESH,
        )

    def pair_copy(ref, sends, lands, j):
        return pltpu.make_async_remote_copy(
            src_ref=ref.at[mz, j], dst_ref=ref.at[mz, j], send_sem=sends.at[j],
            recv_sem=lands.at[j], device_id={"scan": pair}, device_id_type=MESH,
        )

    def evens(body):
        def run(t, carry):
            body(2 * t)
            return carry

        lax.fori_loop(1, n // 2, run, 0)

    pieces = 2 if step % 32 == 0 else 1
    piece = step // pieces

    def send_s(c, u, d):
        first = c * step + u * piece
        return pltpu.make_async_remote_copy(
            src_ref=spectra.at[pl.ds(pl.multiple_of(to(d) * rows + first, piece), piece), :],
            dst_ref=sbuf.at[i, pl.ds(first, piece), :],
            send_sem=s_send.at[c, d], recv_sem=s_recv.at[c, i],
            device_id={"scan": to(d)}, device_id_type=MESH,
        )

    def send_last(u, t):
        p = lax.rem(i + t, n)
        first = (chunks - 1) * step + u * piece
        return pltpu.make_async_remote_copy(
            src_ref=spectra.at[pl.ds(pl.multiple_of(p * rows + first, piece), piece), :],
            dst_ref=sbuf.at[i, pl.ds(first, piece), :],
            send_sem=s_send.at[chunks - 1, t], recv_sem=s_recv.at[chunks - 1, i],
            device_id={"scan": p}, device_id_type=MESH,
        )

    def land_last(t):
        j = lax.rem(i + n - t, n)
        at = pl.ds((chunks - 1) * step, step)
        return pltpu.make_async_remote_copy(
            src_ref=spectra.at[at, :], dst_ref=sbuf.at[j, at, :],
            send_sem=s_send.at[chunks - 1, t], recv_sem=s_recv.at[chunks - 1, j],
            device_id={"scan": lax.rem(i + t, n)}, device_id_type=MESH,
        )

    def land_s(c, d):
        return pltpu.make_async_remote_copy(
            src_ref=spectra.at[pl.ds(c * step, step), :],
            dst_ref=sbuf.at[source(d), pl.ds(c * step, step), :],
            send_sem=s_send.at[c, d], recv_sem=s_recv.at[c, source(d)],
            device_id={"scan": to(d)}, device_id_type=MESH,
        )

    own = pltpu.make_async_copy(
        spectra.at[pl.ds(pl.multiple_of(i * rows, rows), rows), :], sbuf.at[i], own_sem
    )
    own.start()
    pair_copy(hraw, p_send, h_recv, i).start()
    evens(lambda t: column_copy(hraw, h_send, h_recv, t, i).start())
    turn = (2 * lax.rem(i // 2, 2) + mz) * (n - 1) // 4

    def pass_on(t):
        j = along(t)
        column_copy(hraw, h_send, h_recv, t, j).wait_recv()
        pair_copy(hraw, p_send, h_recv, j).start()

    def core_halves(h):
        return pltpu.make_async_remote_copy(
            src_ref=hraw.at[h], dst_ref=hraw.at[h], send_sem=k_sem.at[0], recv_sem=k_sem.at[1],
            device_id={"mz": other}, device_id_type=MESH,
        )

    for c in range(chunks):
        if c == min(1, chunks - 1):
            evens(pass_on)
        for u in range(pieces):
            if c < chunks - 1:
                each(lambda e, c=c, u=u: send_s(c, u, n - 1 - lax.rem(e - 1 + turn, n - 1)).start())
    each(lambda t: [send_last(u, t).start() for u in range(pieces)])

    gacc[...] = jnp.zeros_like(gacc)
    w_across[...] = w_ref[...].T

    def from_other_column(t):
        pair_copy(hraw, p_send, h_recv, along(t)).wait_recv()

    lax.fori_loop(0, n // 2, lambda t, carry: (from_other_column(2 * t + 1), carry)[1], 0)
    core_halves(mz).start()
    core_halves(other).wait_recv()

    def build(block, j):
        now = block(j).astype(F32)
        before = jnp.where(j > 0, block(jnp.maximum(j - 1, 0)).astype(F32), 0.0)
        ext = jnp.concatenate([before, now], 1)
        odd = pltpu.roll(ext, LAG, 1)
        for l in range(LAGS):
            start = width - LANES * (l // 2)
            part = (odd if l % 2 else ext)[:, start : start + width]
            stack[j, l * K : (l + 1) * K, :] = (scale * part).astype(BF16)

    each(lambda j: build(lambda b: jnp.concatenate([hraw[0, b], hraw[1, b]], 1), j), 0)
    own.wait()

    def residual(c, j):
        at = pl.ds(c * step, step)
        recon = jnp.dot(w_ref[at, :], stack[j], preferred_element_type=F32)
        return (recon - sbuf[j, at, :].astype(F32)).astype(BF16)

    groups = width // LANES

    def unit(c, j):
        prods = jnp.dot(
            w_across[:, c * step : (c + 1) * step], residual(c, j), preferred_element_type=F32
        )
        for odd in range(2):
            for q in range(1 - groups, groups):
                terms = []
                for m in range(LAGS // 2):
                    if 0 <= q + m < groups:
                        l = 2 * m + odd
                        terms.append(
                            prods[l * K : (l + 1) * K, (q + m) * LANES : (q + m + 1) * LANES]
                        )
                if not terms:
                    continue
                block = j + 1 if q >= 0 else j
                at = (q % groups) * LANES
                gacc[odd, block, :, at : at + LANES] += functools.reduce(lambda a, b: a + b, terms)

    for c in range(chunks - 1):
        unit(c, i)

        def arrived(d, c=c):
            land_s(c, d).wait_recv()
            unit(c, source(d))

        each(arrived)

    def finish(j):
        after = jnp.concatenate([gacc[1, j + 1], gacc[1, j + 2]], 1)
        g = gacc[0, j + 1] + pltpu.roll(after, 2 * width - LAG, 1)[:, :width]
        gfin[0, j] = g[:, :half]
        gfin[1, j] = g[:, half:]

    def core_copy(j):
        return pltpu.make_async_remote_copy(
            src_ref=gfin.at[other, j], dst_ref=from_core.at[j], send_sem=a_send.at[j],
            recv_sem=a_recv.at[j], device_id={"mz": other}, device_id_type=MESH,
        )

    def send_g(j):
        return pltpu.make_async_remote_copy(
            src_ref=gsum.at[j], dst_ref=from_scan.at[i], send_sem=b_send.at[j],
            recv_sem=b_recv.at[i], device_id={"scan": j}, device_id_type=MESH,
        )

    def land_g(j):
        return pltpu.make_async_remote_copy(
            src_ref=gsum.at[j], dst_ref=from_scan.at[j], send_sem=b_send.at[j],
            recv_sem=b_recv.at[j], device_id={"scan": j}, device_id_type=MESH,
        )

    def pair_sum(j):
        return pltpu.make_async_remote_copy(
            src_ref=gsum.at[j], dst_ref=from_pair.at[j], send_sem=f_send.at[j],
            recv_sem=f_recv.at[j], device_id={"scan": pair}, device_id_type=MESH,
        )

    def add_core(t):
        j = along(n - t)
        core_copy(j).wait_recv()
        gsum[j] = gfin[mz, j] + from_core[j]

        @pl.when(lax.rem(t, 2) == 1)
        def _():
            pair_sum(j).start()

    def add_pair(t):
        j = along(n - t)
        pair_sum(j).wait_recv()
        gsum[j] = gsum[j] + from_pair[j]

    unit(chunks - 1, i)

    def last(t):
        j = lax.rem(i + n - t, n)
        land_last(t).wait_recv()
        unit(chunks - 1, j)
        finish(j)
        core_copy(j).start()

        @pl.when(t > 1)
        def _():
            add_core(t - 1)

        @pl.when(jnp.logical_and(t > 3, lax.rem(t, 2) == 1))
        def _():
            add_pair(t - 3)
            send_g(along(n - t + 3)).start()

    each(last)
    finish(i)
    core_copy(i).start()
    add_core(n - 1)
    add_pair(n - 2)
    send_g(along(2)).start()
    add_core(0)
    add_pair(0)

    def add_scan(d, total):
        j = along(2 * d)
        land_g(j).wait_recv()
        return total + from_scan[j]

    grad = scale * lax.fori_loop(1, n // 2, add_scan, gsum[i])
    act = jnp.where(mz == 0, act[:, :half], act[:, half:])
    new_h = jnp.maximum(act - column(h_rate[...]) * grad, 0.0)
    nh[mz] = new_h
    hn[mz, i] = new_h.astype(BF16)

    def hand_on(j):
        return pltpu.make_async_remote_copy(
            src_ref=hn.at[mz, j], dst_ref=hn.at[mz, j], send_sem=d_send.at[j],
            recv_sem=d_recv.at[j], device_id={"mz": other}, device_id_type=MESH,
        )

    def handed(j):
        return pltpu.make_async_remote_copy(
            src_ref=hn.at[other, j], dst_ref=hn.at[other, j], send_sem=d_send.at[j],
            recv_sem=d_recv.at[j], device_id={"mz": other}, device_id_type=MESH,
        )

    hand_on(i).start()
    pair_copy(hn, q_send, c_recv, i).start()
    evens(lambda t: column_copy(hn, c_send, c_recv, t, i).start())
    e_copy = pltpu.make_async_remote_copy(
        src_ref=nh.at[mz], dst_ref=nh.at[mz], send_sem=e_sem.at[0], recv_sem=e_sem.at[1],
        device_id={"mz": other}, device_id_type=MESH,
    )
    e_copy.start()
    total_w[...] = jnp.zeros_like(total_w)

    def take(t):
        j = along(t)
        pair_copy(hn, q_send, c_recv, j).wait_recv()
        hand_on(j).start()

        @pl.when(lax.rem(t, 2) == 0)
        def _():
            pair_copy(hn, q_send, c_recv, j).start()

    take(1)
    handed(i).wait_recv()

    def second(t, carry):
        j = along(t)

        @pl.when(t + 1 < n)
        def _():
            take(t + 1)

        @pl.when(t < n)
        def _():
            handed(j).wait_recv()

        build(lambda b: jnp.concatenate([hn[0, b], hn[1, b]], 1), j)
        for c in range(chunks):
            total_w[pl.ds(c * step, step), :] += lax.dot_general(
                residual(c, j), stack[j], (((1,), (1,)), ((), ())), preferred_element_type=F32
            )
        return carry

    lax.fori_loop(1, n + 1, second, 0)

    lags = lax.broadcasted_iota(jnp.int32, (K, LAGS * K), 1)
    same = lax.rem(lags, K) == lax.broadcasted_iota(jnp.int32, (K, LAGS * K), 0)
    rates = jnp.sum(jnp.where(same, column(w_rate[...]), 0.0), axis=0, keepdims=True)
    for c in range(chunks):
        at = pl.ds(c * step, step)
        moved = w_ref[at, :].astype(F32) - rates * total_w[at, :]
        w_out[at, :] = moved.astype(BF16)

    e_back = pltpu.make_async_remote_copy(
        src_ref=nh.at[other], dst_ref=nh.at[other], send_sem=e_sem.at[0], recv_sem=e_sem.at[1],
        device_id={"mz": other}, device_id_type=MESH,
    )
    e_back.wait_recv()
    h_out[...] = jnp.concatenate([nh[0], nh[1]], 1)

    evens(lambda t: column_copy(hraw, h_send, h_recv, t, i).wait_send())
    evens(lambda t: column_copy(hn, c_send, c_recv, t, i).wait_send())

    def own_column(t):
        pair_copy(hraw, p_send, h_recv, along(2 * t)).wait_send()
        pair_copy(hn, q_send, c_recv, along(2 * t)).wait_send()
        pair_sum(along(2 * t + 1)).wait_send()

    lax.fori_loop(0, n // 2, lambda t, carry: (own_column(t), carry)[1], 0)
    core_halves(mz).wait_send()
    for c in range(chunks):
        each(lambda d, c=c: land_s(c, d).wait_send())
    evens(lambda t: send_g(along(t)).wait_send())
    each(lambda j: core_copy(j).wait_send(), 0)
    each(lambda j: hand_on(j).wait_send(), 0)
    e_copy.wait_send()


def per_device(n, spectra, templates, activations, h_rate, w_rate):
    rows, cols = templates.shape[1], templates.shape[2]
    width = spectra.shape[1]
    half = width // 2
    chunks = rows // 256 if rows % 256 == 0 else 1
    vmem = pl.BlockSpec(memory_space=pltpu.VMEM)
    dma = pltpu.SemaphoreType.DMA
    new_h, new_w = pl.pallas_call(
        functools.partial(kernel, n, chunks),
        out_shape=(
            jax.ShapeDtypeStruct(activations.shape, F32),
            jax.ShapeDtypeStruct((rows, cols), BF16),
        ),
        in_specs=[pl.BlockSpec(memory_space=pl.ANY), vmem, vmem, vmem, vmem],
        out_specs=(vmem, vmem),
        scratch_shapes=[
            pltpu.VMEM((n, rows, width), BF16),
            pltpu.VMEM((2, n, K, half), BF16),
            pltpu.VMEM((n, cols, width), BF16),
            pltpu.VMEM((2, n + 2, K, width), F32),
            pltpu.VMEM((2, n, K, half), F32),
            pltpu.VMEM((n, K, half), F32),
            pltpu.VMEM((n, K, half), F32),
            pltpu.VMEM((n, K, half), F32),
            pltpu.VMEM((2, K, half), F32),
            pltpu.VMEM((2, n, K, half), BF16),
            pltpu.VMEM((rows, cols), F32),
            pltpu.VMEM((cols, rows), BF16),
            dma,
            dma((chunks, n)),
            dma((chunks, n)),
            dma((n,)),
            dma((n,)),
            dma((n,)),
            dma((n,)),
            dma((n,)),
            dma((n,)),
            dma((n,)),
            dma((n,)),
            dma((n,)),
            dma((n,)),
            dma((n,)),
            dma((n,)),
            dma((n,)),
            dma((2,)),
            dma((2,)),
            pltpu.VMEM((n, K, half), F32),
            dma((n,)),
        ],
        compiler_params=pltpu.CompilerParams(
            collective_id=0, has_side_effects=True, vmem_limit_bytes=56 * 1024 * 1024
        ),
        cost_estimate=pl.CostEstimate(
            flops=8 * n * rows * cols * width, bytes_accessed=4 * n * rows * width, transcendentals=0
        ),
    )(
        spectra,
        templates.reshape(rows, cols),
        activations,
        h_rate.reshape(1, K),
        w_rate.reshape(1, K),
    )
    new_h = jnp.maximum(new_h, 0.0)
    new_w = jnp.maximum(new_w, jnp.zeros((), BF16))
    return new_h, new_w.reshape(templates.shape)


def solution(mesh):
    placed = (
        P("mz", ("slab", "scan")),
        P("mz", ("slab", "scan"), None),
        P(None, ("slab", "scan")),
        P(),
        P(),
    )
    return jax.shard_map(
        functools.partial(per_device, mesh.shape["scan"]),
        mesh=mesh,
        in_specs=placed,
        out_specs=(P(None, ("slab", "scan")), P("mz", ("slab", "scan"), None)),
        check_vma=False,
    )
```

```python
import functools

import jax
import jax.numpy as jnp
from jax import lax
from jax.experimental import pallas as pl
from jax.experimental.pallas import tpu as pltpu
from jax.sharding import PartitionSpec as P

K = 64
LAGS = 8
LAG = 64
LANES = 128
F32 = jnp.float32
BF16 = jnp.bfloat16
MESH = pl.DeviceIdType.MESH


def crossed(a, b, n):
    out, bit = 0, 1
    while bit < n:
        out = out + bit * ((a // bit + b // bit) % 2)
        bit *= 2
    return out


def column(row):
    shape = (K, K)
    same = lax.broadcasted_iota(jnp.int32, shape, 0) == lax.broadcasted_iota(jnp.int32, shape, 1)
    return jnp.sum(jnp.where(same, row, 0.0), axis=1, keepdims=True)


def kernel(
    n, chunks, spectra, w_ref, act_ref, h_rate, w_rate, h_out, w_out,
    sbuf, hraw, stack, gacc, gfin, from_core, gsum, from_scan, nh, hn, total_w, w_across,
    own_sem, s_send, s_recv, h_send, h_recv, a_send, a_recv, b_send, b_recv, c_send, c_recv,
    d_send, d_recv, e_sem, k_sem,
):
    rows, width = sbuf.shape[1], sbuf.shape[2]
    half = width // 2
    step = rows // chunks
    scale = 1.0 / (LAGS * K)
    i = lax.axis_index("scan")
    mz = lax.axis_index("mz")
    other = 1 - mz
    two = n & (n - 1) == 0

    def to(d):
        return crossed(i, d, n) if two else lax.rem(i + d, n)

    def source(d):
        return crossed(i, d, n) if two else lax.rem(i + n - d, n)

    def each(body, start=1):
        def run(d, carry):
            body(d)
            return carry

        lax.fori_loop(start, n, run, 0)

    act = act_ref[...]
    hraw[0, i] = act[:, :half].astype(BF16)
    hraw[1, i] = act[:, half:].astype(BF16)
    barrier = pltpu.get_barrier_semaphore()
    each(lambda d: pl.semaphore_signal(barrier, inc=1, device_id={"scan": to(d)}, device_id_type=MESH))
    pl.semaphore_signal(barrier, inc=1, device_id={"mz": other}, device_id_type=MESH)
    pl.semaphore_wait(barrier, n)

    def send_h(d):
        return pltpu.make_async_remote_copy(
            src_ref=hraw.at[mz, i], dst_ref=hraw.at[mz, i], send_sem=h_send.at[d], recv_sem=h_recv.at[i],
            device_id={"scan": to(d)}, device_id_type=MESH,
        )

    def land_h(d):
        return pltpu.make_async_remote_copy(
            src_ref=hraw.at[mz, source(d)], dst_ref=hraw.at[mz, source(d)], send_sem=h_send.at[d],
            recv_sem=h_recv.at[source(d)], device_id={"scan": to(d)}, device_id_type=MESH,
        )

    pieces = 2 if step % 32 == 0 else 1
    piece = step // pieces

    def send_s(c, u, d):
        first = c * step + u * piece
        return pltpu.make_async_remote_copy(
            src_ref=spectra.at[pl.ds(pl.multiple_of(to(d) * rows + first, piece), piece), :],
            dst_ref=sbuf.at[i, pl.ds(first, piece), :],
            send_sem=s_send.at[c, d], recv_sem=s_recv.at[c, i],
            device_id={"scan": to(d)}, device_id_type=MESH,
        )

    def send_last(u, t):
        p = lax.rem(i + t, n)
        first = (chunks - 1) * step + u * piece
        return pltpu.make_async_remote_copy(
            src_ref=spectra.at[pl.ds(pl.multiple_of(p * rows + first, piece), piece), :],
            dst_ref=sbuf.at[i, pl.ds(first, piece), :],
            send_sem=s_send.at[chunks - 1, t], recv_sem=s_recv.at[chunks - 1, i],
            device_id={"scan": p}, device_id_type=MESH,
        )

    def land_last(t):
        j = lax.rem(i + n - t, n)
        at = pl.ds((chunks - 1) * step, step)
        return pltpu.make_async_remote_copy(
            src_ref=spectra.at[at, :], dst_ref=sbuf.at[j, at, :],
            send_sem=s_send.at[chunks - 1, t], recv_sem=s_recv.at[chunks - 1, j],
            device_id={"scan": lax.rem(i + t, n)}, device_id_type=MESH,
        )

    def land_s(c, d):
        return pltpu.make_async_remote_copy(
            src_ref=spectra.at[pl.ds(c * step, step), :],
            dst_ref=sbuf.at[source(d), pl.ds(c * step, step), :],
            send_sem=s_send.at[c, d], recv_sem=s_recv.at[c, source(d)],
            device_id={"scan": to(d)}, device_id_type=MESH,
        )

    own = pltpu.make_async_copy(
        spectra.at[pl.ds(pl.multiple_of(i * rows, rows), rows), :], sbuf.at[i], own_sem
    )
    own.start()
    each(lambda d: send_h(d).start())
    turn = (2 * lax.rem(i // 2, 2) + mz) * (n - 1) // 4
    for c in range(chunks):
        for u in range(pieces):
            if c < chunks - 1:
                each(lambda e, c=c, u=u: send_s(c, u, n - 1 - lax.rem(e - 1 + turn, n - 1)).start())
    each(lambda t: [send_last(u, t).start() for u in range(pieces)])

    gacc[...] = jnp.zeros_like(gacc)
    w_across[...] = w_ref[...].T
    each(lambda d: land_h(d).wait_recv())

    def core_halves(h):
        return pltpu.make_async_remote_copy(
            src_ref=hraw.at[h], dst_ref=hraw.at[h], send_sem=k_sem.at[0], recv_sem=k_sem.at[1],
            device_id={"mz": other}, device_id_type=MESH,
        )

    core_halves(mz).start()
    core_halves(other).wait_recv()

    def build(block, j):
        now = block(j).astype(F32)
        before = jnp.where(j > 0, block(jnp.maximum(j - 1, 0)).astype(F32), 0.0)
        ext = jnp.concatenate([before, now], 1)
        odd = pltpu.roll(ext, LAG, 1)
        for l in range(LAGS):
            start = width - LANES * (l // 2)
            part = (odd if l % 2 else ext)[:, start : start + width]
            stack[j, l * K : (l + 1) * K, :] = (scale * part).astype(BF16)

    each(lambda j: build(lambda b: jnp.concatenate([hraw[0, b], hraw[1, b]], 1), j), 0)
    own.wait()

    def residual(c, j):
        at = pl.ds(c * step, step)
        recon = jnp.dot(w_ref[at, :], stack[j], preferred_element_type=F32)
        return (recon - sbuf[j, at, :].astype(F32)).astype(BF16)

    groups = width // LANES

    def unit(c, j):
        prods = jnp.dot(
            w_across[:, c * step : (c + 1) * step], residual(c, j), preferred_element_type=F32
        )
        for odd in range(2):
            for q in range(1 - groups, groups):
                terms = []
                for m in range(LAGS // 2):
                    if 0 <= q + m < groups:
                        l = 2 * m + odd
                        terms.append(
                            prods[l * K : (l + 1) * K, (q + m) * LANES : (q + m + 1) * LANES]
                        )
                if not terms:
                    continue
                block = j + 1 if q >= 0 else j
                at = (q % groups) * LANES
                gacc[odd, block, :, at : at + LANES] += functools.reduce(lambda a, b: a + b, terms)

    for c in range(chunks - 1):
        unit(c, i)

        def arrived(d, c=c):
            land_s(c, d).wait_recv()
            unit(c, source(d))

        each(arrived)

    def finish(j):
        after = jnp.concatenate([gacc[1, j + 1], gacc[1, j + 2]], 1)
        g = gacc[0, j + 1] + pltpu.roll(after, 2 * width - LAG, 1)[:, :width]
        gfin[0, j] = g[:, :half]
        gfin[1, j] = g[:, half:]

    def core_copy(j):
        return pltpu.make_async_remote_copy(
            src_ref=gfin.at[other, j], dst_ref=from_core.at[j], send_sem=a_send.at[j],
            recv_sem=a_recv.at[j], device_id={"mz": other}, device_id_type=MESH,
        )

    def send_g(j):
        return pltpu.make_async_remote_copy(
            src_ref=gsum.at[j], dst_ref=from_scan.at[i], send_sem=b_send.at[j],
            recv_sem=b_recv.at[i], device_id={"scan": j}, device_id_type=MESH,
        )

    def land_g(j):
        return pltpu.make_async_remote_copy(
            src_ref=gsum.at[j], dst_ref=from_scan.at[j], send_sem=b_send.at[j],
            recv_sem=b_recv.at[j], device_id={"scan": j}, device_id_type=MESH,
        )

    def add_core(j):
        core_copy(j).wait_recv()
        gsum[j] = gfin[mz, j] + from_core[j]

    def add_and_send(t):
        j = lax.rem(i + n - t, n)
        add_core(j)
        send_g(j).start()

    unit(chunks - 1, i)

    def last(t):
        j = lax.rem(i + n - t, n)
        land_last(t).wait_recv()
        unit(chunks - 1, j)
        finish(j)
        core_copy(j).start()

        @pl.when(t > 1)
        def _():
            add_and_send(t - 1)

    each(last)
    finish(i)
    core_copy(i).start()
    add_and_send(n - 1)
    add_core(i)

    def add_scan(d, total):
        j = lax.rem(i + d, n)
        land_g(j).wait_recv()
        return total + from_scan[j]

    grad = scale * lax.fori_loop(1, n, add_scan, gsum[i])
    act = jnp.where(mz == 0, act[:, :half], act[:, half:])
    new_h = jnp.maximum(act - column(h_rate[...]) * grad, 0.0)
    nh[mz] = new_h
    hn[mz, i] = new_h.astype(BF16)

    def after(t):
        return lax.rem(i + t, n)

    def send_n(t):
        return pltpu.make_async_remote_copy(
            src_ref=hn.at[mz, i], dst_ref=hn.at[mz, i], send_sem=c_send.at[t],
            recv_sem=c_recv.at[i], device_id={"scan": after(n - t)}, device_id_type=MESH,
        )

    def land_n(t):
        return pltpu.make_async_remote_copy(
            src_ref=hn.at[mz, after(t)], dst_ref=hn.at[mz, after(t)], send_sem=c_send.at[t],
            recv_sem=c_recv.at[after(t)], device_id={"scan": after(n - t)}, device_id_type=MESH,
        )

    def hand_on(j):
        return pltpu.make_async_remote_copy(
            src_ref=hn.at[mz, j], dst_ref=hn.at[mz, j], send_sem=d_send.at[j],
            recv_sem=d_recv.at[j], device_id={"mz": other}, device_id_type=MESH,
        )

    def handed(j):
        return pltpu.make_async_remote_copy(
            src_ref=hn.at[other, j], dst_ref=hn.at[other, j], send_sem=d_send.at[j],
            recv_sem=d_recv.at[j], device_id={"mz": other}, device_id_type=MESH,
        )

    hand_on(i).start()
    each(lambda t: send_n(t).start())
    e_copy = pltpu.make_async_remote_copy(
        src_ref=nh.at[mz], dst_ref=nh.at[mz], send_sem=e_sem.at[0], recv_sem=e_sem.at[1],
        device_id={"mz": other}, device_id_type=MESH,
    )
    e_copy.start()
    total_w[...] = jnp.zeros_like(total_w)

    def take(t):
        land_n(t).wait_recv()
        hand_on(after(t)).start()

    take(1)
    handed(i).wait_recv()

    def second(t, carry):
        j = after(t)

        @pl.when(t + 1 < n)
        def _():
            take(t + 1)

        @pl.when(t < n)
        def _():
            handed(j).wait_recv()

        build(lambda b: jnp.concatenate([hn[0, b], hn[1, b]], 1), j)
        for c in range(chunks):
            total_w[pl.ds(c * step, step), :] += lax.dot_general(
                residual(c, j), stack[j], (((1,), (1,)), ((), ())), preferred_element_type=F32
            )
        return carry

    lax.fori_loop(1, n + 1, second, 0)

    lags = lax.broadcasted_iota(jnp.int32, (K, LAGS * K), 1)
    same = lax.rem(lags, K) == lax.broadcasted_iota(jnp.int32, (K, LAGS * K), 0)
    rates = jnp.sum(jnp.where(same, column(w_rate[...]), 0.0), axis=0, keepdims=True)
    for c in range(chunks):
        at = pl.ds(c * step, step)
        moved = w_ref[at, :].astype(F32) - rates * total_w[at, :]
        w_out[at, :] = moved.astype(BF16)

    e_back = pltpu.make_async_remote_copy(
        src_ref=nh.at[other], dst_ref=nh.at[other], send_sem=e_sem.at[0], recv_sem=e_sem.at[1],
        device_id={"mz": other}, device_id_type=MESH,
    )
    e_back.wait_recv()
    h_out[...] = jnp.concatenate([nh[0], nh[1]], 1)

    each(lambda d: send_h(d).wait_send())
    core_halves(mz).wait_send()
    for c in range(chunks):
        each(lambda d, c=c: land_s(c, d).wait_send())
    each(lambda t: send_g(lax.rem(i + t, n)).wait_send())
    each(lambda d: send_n(d).wait_send())
    each(lambda j: core_copy(j).wait_send(), 0)
    each(lambda j: hand_on(j).wait_send(), 0)
    e_copy.wait_send()


def per_device(n, spectra, templates, activations, h_rate, w_rate):
    rows, cols = templates.shape[1], templates.shape[2]
    width = spectra.shape[1]
    half = width // 2
    chunks = rows // 256 if rows % 256 == 0 else 1
    vmem = pl.BlockSpec(memory_space=pltpu.VMEM)
    dma = pltpu.SemaphoreType.DMA
    new_h, new_w = pl.pallas_call(
        functools.partial(kernel, n, chunks),
        out_shape=(
            jax.ShapeDtypeStruct(activations.shape, F32),
            jax.ShapeDtypeStruct((rows, cols), BF16),
        ),
        in_specs=[pl.BlockSpec(memory_space=pl.ANY), vmem, vmem, vmem, vmem],
        out_specs=(vmem, vmem),
        scratch_shapes=[
            pltpu.VMEM((n, rows, width), BF16),
            pltpu.VMEM((2, n, K, half), BF16),
            pltpu.VMEM((n, cols, width), BF16),
            pltpu.VMEM((2, n + 2, K, width), F32),
            pltpu.VMEM((2, n, K, half), F32),
            pltpu.VMEM((n, K, half), F32),
            pltpu.VMEM((n, K, half), F32),
            pltpu.VMEM((n, K, half), F32),
            pltpu.VMEM((2, K, half), F32),
            pltpu.VMEM((2, n, K, half), BF16),
            pltpu.VMEM((rows, cols), F32),
            pltpu.VMEM((cols, rows), BF16),
            dma,
            dma((chunks, n)),
            dma((chunks, n)),
            dma((n,)),
            dma((n,)),
            dma((n,)),
            dma((n,)),
            dma((n,)),
            dma((n,)),
            dma((n,)),
            dma((n,)),
            dma((n,)),
            dma((n,)),
            dma((2,)),
            dma((2,)),
        ],
        compiler_params=pltpu.CompilerParams(
            collective_id=0, has_side_effects=True, vmem_limit_bytes=56 * 1024 * 1024
        ),
        cost_estimate=pl.CostEstimate(
            flops=8 * n * rows * cols * width, bytes_accessed=4 * n * rows * width, transcendentals=0
        ),
    )(
        spectra,
        templates.reshape(rows, cols),
        activations,
        h_rate.reshape(1, K),
        w_rate.reshape(1, K),
    )
    new_h = jnp.maximum(new_h, 0.0)
    new_w = jnp.maximum(new_w, jnp.zeros((), BF16))
    return new_h, new_w.reshape(templates.shape)


def solution(mesh):
    placed = (
        P("mz", ("slab", "scan")),
        P("mz", ("slab", "scan"), None),
        P(None, ("slab", "scan")),
        P(),
        P(),
    )
    return jax.shard_map(
        functools.partial(per_device, mesh.shape["scan"]),
        mesh=mesh,
        in_specs=placed,
        out_specs=(P(None, ("slab", "scan")), P("mz", ("slab", "scan"), None)),
        check_vma=False,
    )
```
